512 devices in a mesh: grp: 32 (over z, core), dev: 16 (over x, y).
Axes of the slice: x: 4, y: 4, z: 16, core: 2. Of those that a mesh axis runs over, the one named last changes fastest.
Arguments:
- source_field: float32 [3, 512, 256, 128], P(None, 'grp', 'dev'), may hold values from -6 to 6
- adjoint_source: float32 [3, 512, 256, 128], P(None, 'grp', 'dev'), may hold values from -6 to 6
- material: int32 [512, 256, 128], P('grp', 'dev'), may hold values from 0 to 3
- density: float32 [512, 128], P('grp'), may hold values from 0 to 1
- eps_inf: float32 [4], replicated, may hold values from 1 to 3
- omega_dt: float32 [4], replicated, may hold values from 0.3 to 1.2
- gamma_dt: float32 [4], replicated, may hold values from 0.2 to 1
- delta_eps: float32 [4], replicated, may hold values from 0.5 to 3
Outputs:
- final_field: float32 [3, 512, 256, 128], P(None, 'grp', 'dev')
- sensitivity: float32 [512, 128], P('grp', 'dev')
The draws below stay inside these ranges and needn't reach their ends.
All inputs are finite; a program needn't handle non-finite values.
Results may differ from the reference program's by a relative error of at most 0.0001.
Values sent between devices are 32-bit elements; how exact they have to be, the bound alone decides.
No kernel may reach another device: no remote copies, remote signals or barrier semaphores. Data moves between devices by JAX's collectives and lax.ppermute only.
A program may use at most 64 MiB of HBM per device.

```python
import math
import jax
import jax.numpy as jnp
from jax import lax

STEPS = 4
MATERIALS = 4
NX = 512
NY = 256
NZ = 128


def set_ends(values, key, smallest, largest):
    dims = values.shape
    spot = [jax.random.randint(jax.random.fold_in(key, axis), (), 0, dims[axis]) for axis in range(len(dims))]
    values = values.at[tuple(spot)].set(smallest)
    longest = dims.index(max(dims))
    spot[longest] = (spot[longest] + 1) % dims[longest]
    return values.at[tuple(spot)].set(largest)


def shard_levels(key, shape, shards, smallest, high):
    def one(dim, shards_of):
        draws = jax.random.uniform(jax.random.fold_in(jax.random.fold_in(key, 6), dim), (shards_of,), jnp.float32, smallest / len(shards), high / len(shards))
        return jnp.repeat(jnp.exp(draws), shape[dim] // shards_of).reshape((-1,) + (1,) * (len(shape) - dim - 1))

    level = one(*shards[0])
    for cut in shards[1:]:
        level = level * one(*cut)
    return level


def gaussian(key, shape, deviation, limit, split=(), held_as=jnp.bfloat16):
    result = deviation * jax.random.normal(key, shape, jnp.float32)
    if split:
        result = result * shard_levels(key, shape, split, -0.22, 0.18)
    return jnp.clip(result, -limit, limit).astype(held_as)


def setup_inputs(seed: int = 0) -> dict:
    key_of = jax.random.split(jax.random.key(seed), 9)
    return {
        "source_field": gaussian(key_of[0], (3, NX, NY, NZ), 1.0, 6.0, ((1, 32), (2, 16)), jnp.float32),
        "adjoint_source": gaussian(key_of[1], (3, NX, NY, NZ), 1.0, 6.0, ((1, 32), (2, 16)), jnp.float32),
        "material": set_ends(jax.random.randint(key_of[2], (NX, NY, NZ), 0, MATERIALS), jax.random.fold_in(key_of[2], 1), 0, MATERIALS - 1).astype(jnp.int32),
        "density": jnp.clip(1.0 * jax.random.uniform(key_of[3], (NX, NZ), jnp.float32) ** shard_levels(key_of[3], (NX, NZ), ((0, 32),), -0.2, 0.2), 0.0, 1.0),
        "eps_inf": jnp.clip(jax.random.uniform(key_of[4], (MATERIALS,), jnp.float32, 1.0, 3.0), 1.0, 3.0),
        "omega_dt": jnp.clip(jax.random.uniform(key_of[5], (MATERIALS,), jnp.float32, 0.3, 1.2), 0.3, 1.2),
        "gamma_dt": jnp.clip(jax.random.uniform(key_of[6], (MATERIALS,), jnp.float32, 0.2, 1.0), 0.2, 1.0),
        "delta_eps": jnp.clip(jax.random.uniform(key_of[7], (MATERIALS,), jnp.float32, 0.5, 3.0), 0.5, 3.0),
    }


courant = 0.5
contrast = 2.0

def ahead(values, along):
    inner = lax.slice_in_dim(values, 1, values.shape[along], axis=along)
    border = jnp.zeros_like(lax.slice_in_dim(values, 0, 1, axis=along))
    return jnp.concatenate([inner, border], along) - values

def behind(values, along):
    inner = lax.slice_in_dim(values, 0, values.shape[along] - 1, axis=along)
    border = jnp.zeros_like(lax.slice_in_dim(values, 0, 1, axis=along))
    return values - jnp.concatenate([border, inner], along)

def pick(material, table):
    summed = jnp.zeros(material.shape, jnp.float32)
    for number in range(MATERIALS):
        summed = summed + jnp.where(material == number, table[number], 0.0)
    return summed

def medium(material, density, eps_inf, omega_dt, gamma_dt, delta_eps):
    squared = pick(material, omega_dt) ** 2
    damping = pick(material, gamma_dt) * 0.5
    gain_now = (2.0 - squared) / (1.0 + damping)
    gain_old = -(1.0 - damping) / (1.0 + damping)
    gain_field = pick(material, delta_eps) * squared / (1.0 + damping)
    inverse = 1.0 / (pick(material, eps_inf) + contrast * density[:, None, :])
    return (gain_now, gain_old, gain_field, inverse)

def advance(state, medium_set):
    electric, magnetic, polar, polar_old = state
    gain_now, gain_old, gain_field, inverse = medium_set
    field_x, field_y, field_z = (electric[0], electric[1], electric[2])
    curl_e = jnp.stack([ahead(field_z, 1) - ahead(field_y, 2), ahead(field_x, 2) - ahead(field_z, 0), ahead(field_y, 0) - ahead(field_x, 1)])
    magnetic = magnetic - courant * curl_e
    magnet_x, magnet_y, magnet_z = (magnetic[0], magnetic[1], magnetic[2])
    curl_h = jnp.stack([behind(magnet_z, 1) - behind(magnet_y, 2), behind(magnet_x, 2) - behind(magnet_z, 0), behind(magnet_y, 0) - behind(magnet_x, 1)])
    update = gain_now * polar + gain_old * polar_old + gain_field * electric
    electric = electric + (courant * curl_h - (update - polar)) * inverse
    return (electric, magnetic, update, polar)

def reference(source_field, adjoint_source, material, density, eps_inf, omega_dt, gamma_dt, delta_eps):
    medium_set = medium(material, density, eps_inf, omega_dt, gamma_dt, delta_eps)
    blank = jnp.zeros_like(source_field)
    forward = (source_field, blank, blank, blank)
    adjoint = (adjoint_source, blank, blank, blank)
    intersection = jnp.zeros((source_field.shape[1], source_field.shape[3]), jnp.float32)
    for number in range(STEPS):
        forward = advance(forward, medium_set)
        adjoint = advance(adjoint, medium_set)
        intersection = intersection + lax.optimization_barrier(jnp.sum(forward[0] * adjoint[0], axis=(0, 2)))
    return (forward[0], intersection * (1.0 / math.sqrt(NY)))
```

```python
import math

import jax
import jax.numpy as jnp
from jax import lax
from jax.experimental import pallas as pl
from jax.experimental.pallas import tpu as pltpu
from jax.sharding import PartitionSpec as P

STEPS = 4
MATERIALS = 4
WIDE = 4
CHUNK = 2
VMEM_LIMIT = 48 * 1024 * 1024


def round_trip(value, axis, steps):
    count = lax.axis_size(axis)
    return lax.ppermute(value, axis, [(s, (s + steps) % count) for s in range(count)])


def iota(dim):
    return lax.broadcasted_iota(jnp.int32, (8, 128), dim)


def turned(value, by, dim):
    return pltpu.roll(value, by % value.shape[dim], dim)


def y_next(tiles):
    last = iota(0) == 7
    rolled = [turned(t, -1, 0) for t in tiles]
    return [jnp.where(last, rolled[(k + 1) % 3], rolled[k]) for k in range(3)]


def y_before(tiles, inside):
    first = iota(0) == 0
    rolled = [turned(t, 1, 0) for t in tiles]
    edge = [rolled[2] * inside, rolled[0], rolled[1]]
    return [jnp.where(first, edge[k], rolled[k]) for k in range(3)]


def z_next(tiles):
    last = iota(1) == 127
    return [jnp.where(last, 0.0, turned(t, -1, 1)) for t in tiles]


def z_before(tiles):
    first = iota(1) == 0
    return [jnp.where(first, 0.0, turned(t, 1, 1)) for t in tiles]


def pack_kernel(source, adjoint, material, density, y_low, y_high, x_low, x_high):
    upper = iota(0) >= 4

    def field(slot, plane, tile):
        if slot < 3:
            return source[slot, plane, tile]
        if slot < 6:
            return adjoint[slot - 3, plane, tile]
        return material[plane, tile].astype(jnp.float32)

    for slot in range(7):
        for pair in range(8):
            even, odd = field(slot, 2 * pair, 0), field(slot, 2 * pair + 1, 0)
            y_low[slot, pair] = jnp.where(upper, turned(odd, 4, 0), even)
            even, odd = field(slot, 2 * pair, 1), field(slot, 2 * pair + 1, 1)
            y_high[slot, pair] = jnp.where(upper, even, turned(odd, 4, 0))
        for plane in range(WIDE):
            for tile in range(2):
                x_low[slot * 8 + plane * 2 + tile] = field(slot, plane, tile)
                x_high[slot * 8 + plane * 2 + tile] = field(slot, 12 + plane, tile)
    x_low[56] = density[0:8]
    x_high[56] = turned(density[8:16], 4, 0)


def corner_kernel(from_next, from_before, halo, c_low, c_high):
    place, count = lax.axis_index("dev"), lax.axis_size("dev")
    upper = iota(0) >= 4
    for slot in range(7):
        for pair in range(8):
            ahead = jnp.where(place < count - 1, from_next[slot, pair], 0.0)
            behind = jnp.where(place > 0, from_before[slot, pair], 0.0)
            even = jnp.where(upper, behind, ahead)
            odd = turned(jnp.where(upper, ahead, behind), 4, 0)
            for plane, value in ((2 * pair, even), (2 * pair + 1, odd)):
                halo[slot, plane] = value
                if plane < WIDE:
                    c_low[slot, plane] = value
                if plane >= 12:
                    c_high[slot, plane - 12] = value


def loop(low, high, body):
    whole = (high - low) // CHUNK
    if whole:

        @pl.loop(0, whole)
        def _(k):
            for u in range(CHUNK):
                body(low + k * CHUNK + u)

    for plane in range(low + whole * CHUNK, high):
        body(plane)


def run_kernel(
    source, adjoint, material, density, halo, from_next, from_before, c_next, c_before,
    eps_inf, omega_dt, gamma_dt, delta_eps,
    final_field, partial, E, H, PA, PB, G, acc,
):
    dev, devs = lax.axis_index("dev"), lax.axis_size("dev")
    grp, grps = lax.axis_index("grp"), lax.axis_size("grp")
    fields = (source, adjoint)

    @pl.loop(0, 16)
    def _(x):
        for run in range(2):
            for c in range(3):
                for tile in range(2):
                    E[run, c, x + WIDE, tile] = fields[run][c, x, tile]
                E[run, c, x + WIDE, 2] = halo[3 * run + c, x]

    @pl.loop(0, WIDE)
    def _(x):
        for run in range(2):
            for c in range(3):
                slot = 3 * run + c
                for main, corner, inside, at in (
                    (from_before, c_before, grp > 0, x),
                    (from_next, c_next, grp < grps - 1, x + 20),
                ):
                    for tile in range(2):
                        E[run, c, at, tile] = jnp.where(inside, main[slot * 8 + x * 2 + tile], 0.0)
                    E[run, c, at, 2] = jnp.where(inside, corner[slot, x], 0.0)

    tables = []
    for m in range(MATERIALS):
        w, g = (jnp.full((8, 128), ref[m], jnp.float32) for ref in (omega_dt, gamma_dt))
        d, e = (jnp.full((8, 128), ref[m], jnp.float32) for ref in (delta_eps, eps_inf))
        squared, damping = w * w, g * 0.5
        tables.append(
            (
                (2.0 - squared) / (1.0 + damping),
                -(1.0 - damping) / (1.0 + damping),
                4.0 * (d * squared / (1.0 + damping)),
                4.0 * e,
            )
        )
    upper = iota(0) >= 4
    y_inside = jnp.where(upper, (dev > 0).astype(jnp.int32), (dev < devs - 1).astype(jnp.int32)) > 0

    def medium(at, tile, number, layer, inside):
        picked = list(tables[0])
        for m in range(1, MATERIALS):
            here = number == m
            picked = [jnp.where(here, t, p) for t, p in zip(tables[m], picked)]
        inverse = 1.0 / (picked[3] + 8.0 * layer)
        if tile == 2:
            inverse = jnp.where(y_inside, inverse, 0.0)
        if inside is not None:
            inverse = jnp.where(inside, inverse, 0.0)
        for k, value in enumerate((picked[0], picked[1], picked[2], inverse)):
            G[k, at, tile] = value

    @pl.loop(0, 16)
    def _(x):
        layer = jnp.broadcast_to(density[pl.ds(x, 1)], (8, 128))
        for tile in range(2):
            medium(x + WIDE, tile, material[x, tile], layer, None)
        medium(x + WIDE, 2, halo[6, x].astype(jnp.int32), layer, None)

    for x in range(WIDE):
        for main, corner, inside, at in (
            (from_before, c_before, grp > 0, x),
            (from_next, c_next, grp < grps - 1, x + 20),
        ):
            layer = jnp.broadcast_to(main[56, x : x + 1], (8, 128))
            for tile in range(2):
                medium(at, tile, main[48 + x * 2 + tile].astype(jnp.int32), layer, inside)
            medium(at, 2, corner[6, x].astype(jnp.int32), layer, inside)

    acc[...] = jnp.zeros_like(acc)
    before_y = jnp.full((8, 128), (dev > 0).astype(jnp.float32))
    before_x = jnp.full((8, 128), (grp > 0).astype(jnp.float32))
    tiles = range(3)

    def load(ref, run, c, at):
        return [ref[run, c, at, t] for t in tiles]

    for step in range(1, STEPS + 1):
        first, last = step == 1, step == STEPS
        low, high = step, 24 - step
        now, old = (PB, PA) if step % 2 == 0 else (PA, PB)

        def magnetic(at):
            for run in range(2):
                ex, ey, ez = (load(E, run, c, at) for c in range(3))
                ey_x, ez_x = (load(E, run, c, at + 1) for c in (1, 2))
                ex_y, ez_y, ex_z, ey_z = y_next(ex), y_next(ez), z_next(ex), z_next(ey)
                for t in tiles:
                    curl = (
                        (ez_y[t] - ez[t]) - (ey_z[t] - ey[t]),
                        (ex_z[t] - ex[t]) - (ez_x[t] - ez[t]),
                        (ey_x[t] - ey[t]) - (ex_y[t] - ex[t]),
                    )
                    for c in range(3):
                        H[run, c, at, t] = -curl[c] if first else H[run, c, at, t] - curl[c]

        def electric(at):
            gains = [[G[k, at, t] for t in tiles] for k in range(4)]
            products = None
            fresh = []
            for run in range(2):
                hx, hy, hz = (load(H, run, c, at) for c in range(3))
                hy_x, hz_x = (load(H, run, c, at - 1) for c in (1, 2))
                hx_y, hz_y = y_before(hx, before_y), y_before(hz, before_y)
                hx_z, hy_z = z_before(hx), z_before(hy)
                mine = []
                for t in range(2) if last else tiles:
                    curl = (
                        (hz[t] - hz_y[t]) - (hy[t] - hy_z[t]),
                        (hx[t] - hx_z[t]) - (hz[t] - hz_x[t]),
                        (hy[t] - hy_x[t]) - (hx[t] - hx_y[t]),
                    )
                    for c in range(3):
                        e = E[run, c, at, t]
                        update = gains[2][t] * e
                        if first:
                            moved = update
                        else:
                            p = old[run, c, at, t]
                            update = gains[0][t] * p + update
                            if step > 2:
                                update = update + gains[1][t] * now[run, c, at, t]
                            moved = update - p
                        e = e + (curl[c] - moved) * gains[3][t]
                        if not last:
                            now[run, c, at, t] = update
                            E[run, c, at, t] = e
                        elif run == 0:
                            final_field[c, at - WIDE, t] = e
                        if t < 2:
                            mine.append(e)
                fresh.append(mine)
            for f, a in zip(*fresh):
                products = f * a if products is None else products + f * a
            return products

        loop(low - 1, high, magnetic)
        for run in range(2):
            for c in (1, 2):
                for t in tiles:
                    H[run, c, WIDE - 1, t] = H[run, c, WIDE - 1, t] * before_x

        def kept(at):
            electric(at)

        def counted(at):
            acc[at - WIDE] += electric(at)

        loop(low, WIDE, kept)
        loop(WIDE, 20, counted)
        loop(20, high, kept)

    partial[...] = jnp.sum(acc[...], axis=1).T


def sum_kernel(scale, received, out):
    out[...] = (jnp.sum(received[...], axis=0) * scale).T


def call(kernel, out_shapes, inputs, scratch=(), tables=0):
    vmem, smem = pl.BlockSpec(memory_space=pltpu.VMEM), pl.BlockSpec(memory_space=pltpu.SMEM)
    return pl.pallas_call(
        kernel,
        out_shape=[jax.ShapeDtypeStruct(s, jnp.float32) for s in out_shapes],
        in_specs=[vmem] * (len(inputs) - tables) + [smem] * tables,
        out_specs=[vmem] * len(out_shapes),
        scratch_shapes=[pltpu.VMEM(s, jnp.float32) for s in scratch],
        compiler_params=pltpu.CompilerParams(vmem_limit_bytes=VMEM_LIMIT),
    )(*inputs)


def on_device(
    source_field, adjoint_source, material, density, eps_inf, omega_dt, gamma_dt, delta_eps
):
    source = source_field.reshape(3, 16, 2, 8, 128)
    adjoint = adjoint_source.reshape(3, 16, 2, 8, 128)
    material = material.reshape(16, 2, 8, 128)
    y_low, y_high, x_low, x_high = call(
        pack_kernel,
        [(7, 8, 8, 128)] * 2 + [(57, 8, 128)] * 2,
        (source, adjoint, material, density),
    )
    y_next_in, y_before_in = round_trip(y_low, "dev", -1), round_trip(y_high, "dev", 1)
    x_next_in, x_before_in = round_trip(x_low, "grp", -1), round_trip(x_high, "grp", 1)
    halo, c_low, c_high = call(
        corner_kernel, [(7, 16, 8, 128)] + [(7, 4, 8, 128)] * 2, (y_next_in, y_before_in)
    )
    c_next_in, c_before_in = round_trip(c_low, "grp", -1), round_trip(c_high, "grp", 1)
    state = (2, 3, 24, 3, 8, 128)
    final_field, partial = call(
        run_kernel,
        [(3, 16, 2, 8, 128), (128, 16)],
        (
            source, adjoint, material, density, halo,
            x_next_in, x_before_in, c_next_in, c_before_in,
            eps_inf, omega_dt, gamma_dt, delta_eps,
        ),
        [state, state, state, state, (4, 24, 3, 8, 128), (16, 8, 128)],
        4,
    )
    received = lax.all_to_all(partial, "dev", split_axis=0, concat_axis=0, tiled=True)
    devs = lax.axis_size("dev")
    across = source_field.shape[2] * devs

    def total(received, out):
        sum_kernel(1.0 / math.sqrt(across), received, out)

    (shared,) = call(total, [(16, 128 // devs)], (received.reshape(devs, 128 // devs, 16),))
    return final_field.reshape(source_field.shape), shared


def solution(mesh):
    in_specs = (
        P(None, "grp", "dev", None),
        P(None, "grp", "dev", None),
        P("grp", "dev", None),
        P("grp", None),
        P(),
        P(),
        P(),
        P(),
    )
    out_specs = (P(None, "grp", "dev", None), P("grp", "dev"))
    return jax.shard_map(
        on_device, mesh=mesh, in_specs=in_specs, out_specs=out_specs, check_vma=False
    )
```

```python
import math

import jax
import jax.numpy as jnp
from jax import lax
from jax.experimental import pallas as pl
from jax.experimental.pallas import tpu as pltpu
from jax.sharding import PartitionSpec as P

STEPS = 4
MATERIALS = 4
WIDE = 4
CHUNK = 2
VMEM_LIMIT = 24 * 1024 * 1024

TILES = range(3)
STATE = (2, 3, 16, 3, 8, 128)


def round_trip(value, axis, steps):
    count = lax.axis_size(axis)
    return lax.ppermute(value, axis, [(s, (s + steps) % count) for s in range(count)])


def iota(dim):
    return lax.broadcasted_iota(jnp.int32, (8, 128), dim)


def turned(value, by, dim):
    return pltpu.roll(value, by % value.shape[dim], dim)


def y_next(tiles):
    last = iota(0) == 7
    rolled = [turned(t, -1, 0) for t in tiles]
    return [jnp.where(last, rolled[(k + 1) % 3], rolled[k]) for k in TILES]


def y_before(tiles, inside):
    first = iota(0) == 0
    rolled = [turned(t, 1, 0) for t in tiles]
    edge = [rolled[2] * inside, rolled[0], rolled[1]]
    return [jnp.where(first, edge[k], rolled[k]) for k in TILES]


def z_next(tiles):
    last = iota(1) == 127
    return [jnp.where(last, 0.0, turned(t, -1, 1)) for t in tiles]


def z_before(tiles):
    first = iota(1) == 0
    return [jnp.where(first, 0.0, turned(t, 1, 1)) for t in tiles]


def loop(low, high, body, chunk=CHUNK):
    whole = (high - low) // chunk
    if whole:

        @pl.loop(0, whole)
        def _(k):
            for u in range(chunk):
                body(low + k * chunk + u)

    for plane in range(low + whole * chunk, high):
        body(plane)


def magnetic_plane(x, first, E, H, put):
    for run in range(2):
        ex, ey, ez = (E(run, c, x) for c in range(3))
        ey_x, ez_x = (E(run, c, x + 1) for c in (1, 2))
        ex_y, ez_y, ex_z, ey_z = y_next(ex), y_next(ez), z_next(ex), z_next(ey)
        olds = None if first else [H(run, c, x) for c in range(3)]
        for t in TILES:
            curl = (
                (ez_y[t] - ez[t]) - (ey_z[t] - ey[t]),
                (ex_z[t] - ex[t]) - (ez_x[t] - ez[t]),
                (ey_x[t] - ey[t]) - (ex_y[t] - ex[t]),
            )
            for c in range(3):
                put(run, c, x, t, -curl[c] if first else olds[c][t] - curl[c])


def electric_plane(x, step, E, H, now, old, gains, before_y, put_e, put_p):
    first, last = step == 1, step == STEPS
    fresh = []
    for run in range(2):
        hx, hy, hz = (H(run, c, x) for c in range(3))
        hy_x, hz_x = (H(run, c, x - 1) for c in (1, 2))
        hx_y, hz_y = y_before(hx, before_y), y_before(hz, before_y)
        hx_z, hy_z = z_before(hx), z_before(hy)
        es = [E(run, c, x) for c in range(3)]
        ps = None if first else [old(run, c, x) for c in range(3)]
        qs = None if step <= 2 else [now(run, c, x) for c in range(3)]
        mine = []
        for t in range(2) if last else TILES:
            curl = (
                (hz[t] - hz_y[t]) - (hy[t] - hy_z[t]),
                (hx[t] - hx_z[t]) - (hz[t] - hz_x[t]),
                (hy[t] - hy_x[t]) - (hx[t] - hx_y[t]),
            )
            for c in range(3):
                update = gains[2][t] * es[c][t]
                if first:
                    moved = update
                else:
                    update = gains[0][t] * ps[c][t] + update
                    if step > 2:
                        update = update + gains[1][t] * qs[c][t]
                    moved = update - ps[c][t]
                e = es[c][t] + (curl[c] - moved) * gains[3][t]
                put_e(run, c, x, t, e)
                if not last:
                    put_p(run, c, x, t, update)
                if t < 2:
                    mine.append(e)
        fresh.append(mine)
    products = None
    for f, a in zip(*fresh):
        products = f * a if products is None else products + f * a
    return products


def tables_of(eps_inf, omega_dt, gamma_dt, delta_eps):
    tables = []
    for m in range(MATERIALS):
        w, g = (jnp.full((8, 128), ref[m], jnp.float32) for ref in (omega_dt, gamma_dt))
        d, e = (jnp.full((8, 128), ref[m], jnp.float32) for ref in (delta_eps, eps_inf))
        squared, damping = w * w, g * 0.5
        tables.append(
            (
                (2.0 - squared) / (1.0 + damping),
                -(1.0 - damping) / (1.0 + damping),
                4.0 * (d * squared / (1.0 + damping)),
                4.0 * e,
            )
        )
    return tables


def medium(tables, number, layer, inside=None):
    picked = list(tables[0])
    for m in range(1, MATERIALS):
        here = number == m
        picked = [jnp.where(here, t, p) for t, p in zip(tables[m], picked)]
    inverse = 1.0 / (picked[3] + 8.0 * layer)
    if inside is not None:
        inverse = jnp.where(inside, inverse, 0.0)
    return picked[0], picked[1], picked[2], inverse


def y_inside(dev, devs):
    above, below = (dev < devs - 1).astype(jnp.int32), (dev > 0).astype(jnp.int32)
    return jnp.where(iota(0) >= 4, below, above) > 0


def layer_of(ref, *index):
    return jnp.broadcast_to(ref[index], (8, 128))


def pack_kernel(
    source_hbm, adjoint_hbm, material_hbm, density_hbm,
    y_low, y_high, x_low, x_high, source, adjoint, material, density, sems,
):
    pairs = ((source_hbm, source), (adjoint_hbm, adjoint), (material_hbm, material), (density_hbm, density))
    copies = [pltpu.make_async_copy(s, d, sems.at[k]) for k, (s, d) in enumerate(pairs)]
    for copy in copies:
        copy.start()
    for copy in copies:
        copy.wait()
    upper = iota(0) >= 4

    def field(slot, plane, tile):
        if slot < 3:
            return source[slot, plane, tile]
        if slot < 6:
            return adjoint[slot - 3, plane, tile]
        return material[plane, tile].astype(jnp.float32)

    for slot in range(7):
        for pair in range(8):
            even, odd = field(slot, 2 * pair, 0), field(slot, 2 * pair + 1, 0)
            y_low[slot, pair] = jnp.where(upper, turned(odd, 4, 0), even)
            even, odd = field(slot, 2 * pair, 1), field(slot, 2 * pair + 1, 1)
            y_high[slot, pair] = jnp.where(upper, even, turned(odd, 4, 0))
        for plane in range(WIDE):
            for tile in range(2):
                x_low[slot * 8 + plane * 2 + tile] = field(slot, plane, tile)
                x_high[slot * 8 + plane * 2 + tile] = field(slot, 12 + plane, tile)
    x_low[56] = density[0:8]
    x_high[56] = turned(density[8:16], 4, 0)


def medium_kernel(material, density, eps_inf, omega_dt, gamma_dt, delta_eps, G):
    tables = tables_of(eps_inf, omega_dt, gamma_dt, delta_eps)

    @pl.loop(0, 16)
    def _(x):
        layer = layer_of(density, pl.ds(x, 1))
        for tile in range(2):
            for k, value in enumerate(medium(tables, material[x, tile], layer)):
                G[k, x, tile] = value


def corner_kernel(place, count, from_next, from_before, halo, c_low, c_high):
    upper = iota(0) >= 4
    for slot in range(7):
        for pair in range(8):
            ahead = jnp.where(place < count - 1, from_next[slot, pair], 0.0)
            behind = jnp.where(place > 0, from_before[slot, pair], 0.0)
            even = jnp.where(upper, behind, ahead)
            odd = turned(jnp.where(upper, ahead, behind), 4, 0)
            for plane, value in ((2 * pair, even), (2 * pair + 1, odd)):
                halo[slot, plane] = value
                if plane < WIDE:
                    c_low[slot, plane] = value
                if plane >= 12:
                    c_high[slot, plane - 12] = value


def inner_kernel(
    dev, devs,
    source, adjoint, halo, density, G, eps_inf, omega_dt, gamma_dt, delta_eps,
    E, H, PA, PB, G2, acc,
):
    tables = tables_of(eps_inf, omega_dt, gamma_dt, delta_eps)
    inside = y_inside(dev, devs)
    fields = (source, adjoint)

    @pl.loop(0, 16)
    def _(x):
        for run in range(2):
            for c in range(3):
                for tile in range(2):
                    E[run, c, x, tile] = fields[run][c, x, tile]
                E[run, c, x, 2] = halo[3 * run + c, x]
        layer = layer_of(density, pl.ds(x, 1))
        for k, value in enumerate(medium(tables, halo[6, x].astype(jnp.int32), layer, inside)):
            G2[k, x] = value

    acc[...] = jnp.zeros_like(acc)
    before_y = jnp.full((8, 128), (dev > 0).astype(jnp.float32))

    def reader(ref):
        return lambda run, c, x: [ref[run, c, x, t] for t in TILES]

    def writer(ref):
        def put(run, c, x, t, value):
            ref[run, c, x, t] = value

        return put

    for step in range(1, STEPS + 1):
        now, old = (PB, PA) if step % 2 == 0 else (PA, PB)

        def magnetic(x):
            magnetic_plane(x, step == 1, reader(E), reader(H), writer(H))

        def electric(x):
            gains = [[G[k, x, 0], G[k, x, 1], G2[k, x]] for k in range(4)]
            acc[x] += electric_plane(
                x, step, reader(E), reader(H), reader(now), reader(old), gains, before_y, writer(E), writer(now)
            )

        loop(step - 1, 16 - step, magnetic)
        loop(step, 16 - step, electric)


def outer_kernel(
    dev, devs, grp, grps,
    E_in, H_in, PA_in, PB_in, G, G2, acc,
    from_next, from_before, c_next, c_before, eps_inf, omega_dt, gamma_dt, delta_eps,
    final_field, partial, E, H, PA, PB, GO, sums,
):
    tables = tables_of(eps_inf, omega_dt, gamma_dt, delta_eps)
    y_in = y_inside(dev, devs)
    before_y = jnp.full((8, 128), (dev > 0).astype(jnp.float32))
    before_x = jnp.full((8, 128), (grp > 0).astype(jnp.float32))
    low_in, high_in = grp > 0, grp < grps - 1

    def slot_of(x):
        return x + 4 if x < 8 else x - 3

    for side in range(2):
        main, corner, x_in = ((from_before, c_before, low_in), (from_next, c_next, high_in))[side]
        for k in range(WIDE):
            x = 16 * side + k - (0 if side else 4)
            layer = layer_of(main, 56, pl.ds(k, 1))
            for t in TILES:
                number = corner[6, k] if t == 2 else main[48 + k * 2 + t]
                ok = jnp.logical_and(y_in, x_in) if t == 2 else x_in
                for n, value in enumerate(medium(tables, number.astype(jnp.int32), layer, ok)):
                    GO[n, side * 4 + k, t] = value

    def start(run, c, x):
        main, corner, x_in, k = (from_before, c_before, low_in, x + 4) if x < 0 else (from_next, c_next, high_in, x - 16)
        slot = 3 * run + c
        tiles = [main[slot * 8 + k * 2 + t] for t in range(2)] + [corner[slot, k]]
        return [jnp.where(x_in, t, 0.0) for t in tiles]

    for step in range(1, STEPS + 1):
        now, old, now_in, old_in = (PB, PA, PB_in, PA_in) if step % 2 == 0 else (PA, PB, PA_in, PB_in)

        def reader(mine, theirs, x_low, x_high):
            def read(run, c, x):
                if x_low <= x < x_high:
                    return [theirs[run, c, x, t] for t in TILES]
                if mine is E and step == 1:
                    return start(run, c, x)
                return [mine[run, c, slot_of(x), t] for t in TILES]

            return read

        def writer(ref):
            def put(run, c, x, t, value):
                ref[run, c, slot_of(x), t] = value

            return put

        def put_final(run, c, x, t, value):
            if run == 0:
                final_field[c, x, t] = value

        read_e = reader(E, E_in, step - 1, 17 - step)
        h_before = reader(H, H_in, max(step - 2, 0), 17 - step)
        h_after = reader(H, H_in, step - 1, 16 - step)
        read_now, read_old = reader(now, now_in, step - 2, 18 - step), reader(old, old_in, step - 1, 17 - step)

        for x in (*range(step - 5, step - 1), *range(16 - step, 20 - step)):
            magnetic_plane(x, step == 1, read_e, h_before, writer(H))
        for run in range(2):
            for c in (1, 2):
                for t in TILES:
                    H[run, c, slot_of(-1), t] = H[run, c, slot_of(-1), t] * before_x
        for x in (*range(step - 4, step), *range(16 - step, 20 - step)):
            if 0 <= x < 16:
                gains = [[G[k, x, 0], G[k, x, 1], G2[k, x]] for k in range(4)]
            else:
                gains = [[GO[k, x + 4 if x < 0 else x - 12, t] for t in TILES] for k in range(4)]
            put_e = put_final if step == STEPS else writer(E)
            products = electric_plane(
                x, step, read_e, h_after, read_now, read_old, gains, before_y, put_e, writer(now)
            )
            if 0 <= x < 16:
                k = x if x < 8 else x - 8
                sums[k] = products + (acc[x] if step in (x + 1, 16 - x) else sums[k])

    for c in range(3):
        for x in range(4, 12):
            for t in range(2):
                final_field[c, x, t] = E_in[0, c, x, t]

    whole = jnp.concatenate([sums[0:4], acc[4:12], sums[4:8]], axis=0)
    table = jnp.concatenate([jnp.sum(whole, axis=1), jnp.zeros((112, 128), jnp.float32)], axis=0)
    blocks = table.T.reshape(16, 8, 128)
    partial[...] = jnp.sum(pltpu.roll(blocks, 0, 2, stride=16, stride_axis=1), axis=1)


def sum_kernel(scale, received, out):
    row = jnp.broadcast_to(jnp.sum(received[...], axis=0, keepdims=True) * scale, (8, 128))
    table = row
    for z in range(1, 8):
        table = jnp.where(iota(0) == z, turned(row, -16 * z, 1), table)
    out[...] = table[:, 0:16]


def call(kernel, out_shapes, inputs, scratch=(), tables=0, hbm=False):
    vmem, smem = pl.BlockSpec(memory_space=pltpu.VMEM), pl.BlockSpec(memory_space=pltpu.SMEM)
    where = pl.BlockSpec(memory_space=pltpu.HBM) if hbm else vmem
    return pl.pallas_call(
        kernel,
        out_shape=[jax.ShapeDtypeStruct(s, jnp.float32) for s in out_shapes],
        in_specs=[where] * (len(inputs) - tables) + [smem] * tables,
        out_specs=[vmem] * len(out_shapes),
        scratch_shapes=[s if not isinstance(s, tuple) else pltpu.VMEM(s, jnp.float32) for s in scratch],
        compiler_params=pltpu.CompilerParams(vmem_limit_bytes=VMEM_LIMIT),
    )(*inputs)


def placed(kernel, *axes):
    def with_place(*refs):
        where = [f(a) for a in axes for f in (lax.axis_index, lax.axis_size)]
        kernel(*where, *refs)

    return with_place


def on_device(
    source_field, adjoint_source, material, density, eps_inf, omega_dt, gamma_dt, delta_eps
):
    source = source_field.reshape(3, 16, 2, 8, 128)
    adjoint = adjoint_source.reshape(3, 16, 2, 8, 128)
    material = material.reshape(16, 2, 8, 128)
    params = (eps_inf, omega_dt, gamma_dt, delta_eps)
    y_low, y_high, x_low, x_high = call(
        pack_kernel,
        [(7, 8, 8, 128)] * 2 + [(57, 8, 128)] * 2,
        (source, adjoint, material, density),
        [
            source.shape, adjoint.shape, pltpu.VMEM(material.shape, jnp.int32), density.shape,
            pltpu.SemaphoreType.DMA((4,)),
        ],
        hbm=True,
    )
    y_next_in, y_before_in = round_trip(y_low, "dev", -1), round_trip(y_high, "dev", 1)
    x_next_in, x_before_in = round_trip(x_low, "grp", -1), round_trip(x_high, "grp", 1)
    (gains,) = call(medium_kernel, [(4, 16, 2, 8, 128)], (material, density, *params), tables=4)
    halo, c_low, c_high = call(
        placed(corner_kernel, "dev"),
        [(7, 16, 8, 128)] + [(7, 4, 8, 128)] * 2,
        (y_next_in, y_before_in),
    )
    c_next_in, c_before_in = round_trip(c_low, "grp", -1), round_trip(c_high, "grp", 1)
    state = call(
        placed(inner_kernel, "dev"),
        [STATE] * 4 + [(4, 16, 8, 128), (16, 8, 128)],
        (source, adjoint, halo, density, gains, *params),
        tables=4,
    )
    *fields, halo_gains, acc = state
    outer = (2, 3, 17, 3, 8, 128)
    final_field, partial = call(
        placed(outer_kernel, "dev", "grp"),
        [(3, 16, 2, 8, 128), (16, 128)],
        (
            *fields, gains, halo_gains, acc,
            x_next_in, x_before_in, c_next_in, c_before_in, *params,
        ),
        [outer] * 4 + [(4, 8, 3, 8, 128), (8, 8, 128)],
        4,
    )
    received = lax.all_to_all(partial, "dev", split_axis=0, concat_axis=0, tiled=True)
    across = source_field.shape[2] * lax.axis_size("dev")

    def total(received, out):
        sum_kernel(1.0 / math.sqrt(across), received, out)

    (shared,) = call(total, [(8, 16)], (received,))
    return final_field.reshape(source_field.shape), shared.T


def solution(mesh):
    in_specs = (
        P(None, "grp", "dev", None),
        P(None, "grp", "dev", None),
        P("grp", "dev", None),
        P("grp", None),
        P(),
        P(),
        P(),
        P(),
    )
    out_specs = (P(None, "grp", "dev", None), P("grp", "dev"))
    return jax.shard_map(
        on_device, mesh=mesh, in_specs=in_specs, out_specs=out_specs, check_vma=False
    )
```

```python
import math

import jax
import jax.numpy as jnp
from jax import lax
from jax.experimental import pallas as pl
from jax.experimental.pallas import tpu as pltpu
from jax.sharding import PartitionSpec as P

STEPS = 4
MATERIALS = 4
WIDE = 4
CHUNK = 4
VMEM_LIMIT = 24 * 1024 * 1024

TILES = range(3)
STATE = (2, 3, 16, 3, 8, 128)


def round_trip(value, axis, steps):
    count = lax.axis_size(axis)
    return lax.ppermute(value, axis, [(s, (s + steps) % count) for s in range(count)])


def iota(dim):
    return lax.broadcasted_iota(jnp.int32, (8, 128), dim)


def turned(value, by, dim):
    return pltpu.roll(value, by % value.shape[dim], dim)


def y_next(tiles):
    last = iota(0) == 7
    rolled = [turned(t, -1, 0) for t in tiles]
    return [jnp.where(last, rolled[(k + 1) % 3], rolled[k]) for k in TILES]


def y_before(tiles, inside):
    first = iota(0) == 0
    rolled = [turned(t, 1, 0) for t in tiles]
    edge = [rolled[2] * inside, rolled[0], rolled[1]]
    return [jnp.where(first, edge[k], rolled[k]) for k in TILES]


def z_next(tiles):
    last = iota(1) == 127
    return [jnp.where(last, 0.0, turned(t, -1, 1)) for t in tiles]


def z_before(tiles):
    first = iota(1) == 0
    return [jnp.where(first, 0.0, turned(t, 1, 1)) for t in tiles]


def loop(low, high, body, chunk=CHUNK):
    whole = (high - low) // chunk
    if whole:

        @pl.loop(0, whole)
        def _(k):
            for u in range(chunk):
                body(low + k * chunk + u)

    for plane in range(low + whole * chunk, high):
        body(plane)


def magnetic_plane(x, first, E, H, put):
    for run in range(2):
        ex, ey, ez = (E(run, c, x) for c in range(3))
        ey_x, ez_x = (E(run, c, x + 1) for c in (1, 2))
        ex_y, ez_y, ex_z, ey_z = y_next(ex), y_next(ez), z_next(ex), z_next(ey)
        olds = None if first else [H(run, c, x) for c in range(3)]
        for t in TILES:
            curl = (
                (ez_y[t] - ez[t]) - (ey_z[t] - ey[t]),
                (ex_z[t] - ex[t]) - (ez_x[t] - ez[t]),
                (ey_x[t] - ey[t]) - (ex_y[t] - ex[t]),
            )
            for c in range(3):
                put(run, c, x, t, -curl[c] if first else olds[c][t] - curl[c])


def electric_plane(x, step, E, H, now, old, gains, before_y, put_e, put_p):
    first, last = step == 1, step == STEPS
    fresh = []
    for run in range(2):
        hx, hy, hz = (H(run, c, x) for c in range(3))
        hy_x, hz_x = (H(run, c, x - 1) for c in (1, 2))
        hx_y, hz_y = y_before(hx, before_y), y_before(hz, before_y)
        hx_z, hy_z = z_before(hx), z_before(hy)
        es = [E(run, c, x) for c in range(3)]
        ps = None if first else [old(run, c, x) for c in range(3)]
        qs = None if step <= 2 else [now(run, c, x) for c in range(3)]
        mine = []
        for t in range(2) if last else TILES:
            curl = (
                (hz[t] - hz_y[t]) - (hy[t] - hy_z[t]),
                (hx[t] - hx_z[t]) - (hz[t] - hz_x[t]),
                (hy[t] - hy_x[t]) - (hx[t] - hx_y[t]),
            )
            for c in range(3):
                update = gains[2][t] * es[c][t]
                if first:
                    moved = update
                else:
                    update = gains[0][t] * ps[c][t] + update
                    if step > 2:
                        update = update + gains[1][t] * qs[c][t]
                    moved = update - ps[c][t]
                e = es[c][t] + (curl[c] - moved) * gains[3][t]
                put_e(run, c, x, t, e)
                if not last:
                    put_p(run, c, x, t, update)
                if t < 2:
                    mine.append(e)
        fresh.append(mine)
    products = None
    for f, a in zip(*fresh):
        products = f * a if products is None else products + f * a
    return products


def tables_of(eps_inf, omega_dt, gamma_dt, delta_eps):
    tables = []
    for m in range(MATERIALS):
        w, g = (jnp.full((8, 128), ref[m], jnp.float32) for ref in (omega_dt, gamma_dt))
        d, e = (jnp.full((8, 128), ref[m], jnp.float32) for ref in (delta_eps, eps_inf))
        squared, damping = w * w, g * 0.5
        tables.append(
            (
                (2.0 - squared) / (1.0 + damping),
                -(1.0 - damping) / (1.0 + damping),
                4.0 * (d * squared / (1.0 + damping)),
                4.0 * e,
            )
        )
    return tables


def medium(tables, number, layer, inside=None):
    picked = list(tables[0])
    for m in range(1, MATERIALS):
        here = number == m
        picked = [jnp.where(here, t, p) for t, p in zip(tables[m], picked)]
    inverse = 1.0 / (picked[3] + 8.0 * layer)
    if inside is not None:
        inverse = jnp.where(inside, inverse, 0.0)
    return picked[0], picked[1], picked[2], inverse


def y_inside(dev, devs):
    above, below = (dev < devs - 1).astype(jnp.int32), (dev > 0).astype(jnp.int32)
    return jnp.where(iota(0) >= 4, below, above) > 0


def layer_of(ref, *index):
    return jnp.broadcast_to(ref[index], (8, 128))


def pack_kernel(
    source_hbm, adjoint_hbm, material_hbm, density_hbm,
    y_low, y_high, source, adjoint, material, density, sems,
):
    pairs = ((source_hbm, source), (adjoint_hbm, adjoint), (material_hbm, material), (density_hbm, density))
    copies = [pltpu.make_async_copy(s, d, sems.at[k]) for k, (s, d) in enumerate(pairs)]
    for copy in copies:
        copy.start()
    for copy in copies:
        copy.wait()
    upper = iota(0) >= 4
    for slot in range(7):
        for pair in range(8):
            even, odd = (field_of(source, adjoint, material, slot, 2 * pair + k, 0) for k in range(2))
            y_low[slot, pair] = jnp.where(upper, turned(odd, 4, 0), even)
            even, odd = (field_of(source, adjoint, material, slot, 2 * pair + k, 1) for k in range(2))
            y_high[slot, pair] = jnp.where(upper, even, turned(odd, 4, 0))


def field_of(source, adjoint, material, slot, plane, tile):
    if slot < 3:
        return source[slot, plane, tile]
    if slot < 6:
        return adjoint[slot - 3, plane, tile]
    return material[plane, tile].astype(jnp.float32)


def medium_kernel(material, density, eps_inf, omega_dt, gamma_dt, delta_eps, G):
    tables = tables_of(eps_inf, omega_dt, gamma_dt, delta_eps)

    @pl.loop(0, 16)
    def _(x):
        layer = layer_of(density, pl.ds(x, 1))
        for tile in range(2):
            for k, value in enumerate(medium(tables, material[x, tile], layer)):
                G[k, x, tile] = value


def edge_kernel(
    place, count, from_next, from_before, source, adjoint, material, density, halo, x_low, x_high
):
    upper = iota(0) >= 4
    for slot in range(7):
        for pair in range(8):
            ahead = jnp.where(place < count - 1, from_next[slot, pair], 0.0)
            behind = jnp.where(place > 0, from_before[slot, pair], 0.0)
            even = jnp.where(upper, behind, ahead)
            odd = turned(jnp.where(upper, ahead, behind), 4, 0)
            for plane, value in ((2 * pair, even), (2 * pair + 1, odd)):
                halo[slot, plane] = value
                if not WIDE <= plane < 12:
                    to, k = (x_low, plane) if plane < WIDE else (x_high, plane - 12)
                    for tile in range(2):
                        to[slot * 12 + k * 3 + tile] = field_of(source, adjoint, material, slot, plane, tile)
                    to[slot * 12 + k * 3 + 2] = value
    x_low[84] = density[0:8]
    x_high[84] = turned(density[8:16], 4, 0)


def inner_kernel(
    dev, devs,
    source, adjoint, halo, density, G, eps_inf, omega_dt, gamma_dt, delta_eps,
    E, H, PA, PB, G2, acc,
):
    tables = tables_of(eps_inf, omega_dt, gamma_dt, delta_eps)
    inside = y_inside(dev, devs)
    fields = (source, adjoint)

    @pl.loop(0, 16)
    def _(x):
        for run in range(2):
            for c in range(3):
                for tile in range(2):
                    E[run, c, x, tile] = fields[run][c, x, tile]
                E[run, c, x, 2] = halo[3 * run + c, x]
        layer = layer_of(density, pl.ds(x, 1))
        for k, value in enumerate(medium(tables, halo[6, x].astype(jnp.int32), layer, inside)):
            G2[k, x] = value

    acc[...] = jnp.zeros_like(acc)
    before_y = jnp.full((8, 128), (dev > 0).astype(jnp.float32))

    def reader(ref):
        return lambda run, c, x: [ref[run, c, x, t] for t in TILES]

    def writer(ref):
        def put(run, c, x, t, value):
            ref[run, c, x, t] = value

        return put

    for step in range(1, STEPS + 1):
        now, old = (PB, PA) if step % 2 == 0 else (PA, PB)

        def magnetic(x):
            magnetic_plane(x, step == 1, reader(E), reader(H), writer(H))

        def electric(x):
            gains = [[G[k, x, 0], G[k, x, 1], G2[k, x]] for k in range(4)]
            acc[x] += electric_plane(
                x, step, reader(E), reader(H), reader(now), reader(old), gains, before_y, writer(E), writer(now)
            )

        loop(step - 1, 16 - step, magnetic)
        loop(step, 16 - step, electric)


def outer_kernel(
    dev, devs, grp, grps,
    E_in, H_in, PA_in, PB_in, G, G2, acc,
    from_next, from_before, eps_inf, omega_dt, gamma_dt, delta_eps,
    final_field, partial, E, H, PA, PB, GO, sums,
):
    tables = tables_of(eps_inf, omega_dt, gamma_dt, delta_eps)
    y_in = y_inside(dev, devs)
    before_y = jnp.full((8, 128), (dev > 0).astype(jnp.float32))
    before_x = jnp.full((8, 128), (grp > 0).astype(jnp.float32))
    low_in, high_in = grp > 0, grp < grps - 1

    def slot_of(x):
        return x + 4 if x < 8 else x - 3

    for side in range(2):
        main, x_in = ((from_before, low_in), (from_next, high_in))[side]
        for k in range(WIDE):
            x = 16 * side + k - (0 if side else 4)
            layer = layer_of(main, 84, pl.ds(k, 1))
            for t in TILES:
                number = main[72 + k * 3 + t]
                ok = jnp.logical_and(y_in, x_in) if t == 2 else x_in
                for n, value in enumerate(medium(tables, number.astype(jnp.int32), layer, ok)):
                    GO[n, side * 4 + k, t] = value

    def start(run, c, x):
        main, x_in, k = (from_before, low_in, x + 4) if x < 0 else (from_next, high_in, x - 16)
        return [jnp.where(x_in, main[(3 * run + c) * 12 + k * 3 + t], 0.0) for t in TILES]

    for step in range(1, STEPS + 1):
        now, old, now_in, old_in = (PB, PA, PB_in, PA_in) if step % 2 == 0 else (PA, PB, PA_in, PB_in)

        def reader(mine, theirs, x_low, x_high):
            def read(run, c, x):
                if x_low <= x < x_high:
                    return [theirs[run, c, x, t] for t in TILES]
                if mine is E and step == 1:
                    return start(run, c, x)
                return [mine[run, c, slot_of(x), t] for t in TILES]

            return read

        def writer(ref):
            def put(run, c, x, t, value):
                ref[run, c, slot_of(x), t] = value

            return put

        def put_final(run, c, x, t, value):
            if run == 0:
                final_field[c, x, t] = value

        read_e = reader(E, E_in, step - 1, 17 - step)
        h_before = reader(H, H_in, max(step - 2, 0), 17 - step)
        h_after = reader(H, H_in, step - 1, 16 - step)
        read_now, read_old = reader(now, now_in, step - 2, 18 - step), reader(old, old_in, step - 1, 17 - step)

        for x in (*range(step - 5, step - 1), *range(16 - step, 20 - step)):
            magnetic_plane(x, step == 1, read_e, h_before, writer(H))
        for run in range(2):
            for c in (1, 2):
                for t in TILES:
                    H[run, c, slot_of(-1), t] = H[run, c, slot_of(-1), t] * before_x
        for x in (*range(step - 4, step), *range(16 - step, 20 - step)):
            if 0 <= x < 16:
                gains = [[G[k, x, 0], G[k, x, 1], G2[k, x]] for k in range(4)]
            else:
                gains = [[GO[k, x + 4 if x < 0 else x - 12, t] for t in TILES] for k in range(4)]
            put_e = put_final if step == STEPS else writer(E)
            products = electric_plane(
                x, step, read_e, h_after, read_now, read_old, gains, before_y, put_e, writer(now)
            )
            if 0 <= x < 16:
                k = x if x < 8 else x - 8
                sums[k] = products + (acc[x] if step in (x + 1, 16 - x) else sums[k])

    for c in range(3):
        for x in range(4, 12):
            for t in range(2):
                final_field[c, x, t] = E_in[0, c, x, t]

    whole = jnp.concatenate([sums[0:4], acc[4:12], sums[4:8]], axis=0)
    table = jnp.concatenate([jnp.sum(whole, axis=1), jnp.zeros((112, 128), jnp.float32)], axis=0)
    blocks = table.T.reshape(16, 8, 128)
    partial[...] = jnp.sum(pltpu.roll(blocks, 0, 2, stride=16, stride_axis=1), axis=1)


def sum_kernel(scale, received, out):
    row = jnp.broadcast_to(jnp.sum(received[...], axis=0, keepdims=True) * scale, (8, 128))
    table = row
    for z in range(1, 8):
        table = jnp.where(iota(0) == z, turned(row, -16 * z, 1), table)
    out[...] = table[:, 0:16]


def call(kernel, out_shapes, inputs, scratch=(), tables=0, hbm=False):
    vmem, smem = pl.BlockSpec(memory_space=pltpu.VMEM), pl.BlockSpec(memory_space=pltpu.SMEM)
    where = pl.BlockSpec(memory_space=pltpu.HBM) if hbm else vmem
    if hbm:
        inputs = [pltpu.with_memory_space_constraint(x, pltpu.HBM) for x in inputs]
    return pl.pallas_call(
        kernel,
        out_shape=[jax.ShapeDtypeStruct(s, jnp.float32) if isinstance(s, tuple) else s for s in out_shapes],
        in_specs=[where] * (len(inputs) - tables) + [smem] * tables,
        out_specs=[vmem] * len(out_shapes),
        scratch_shapes=[s if not isinstance(s, tuple) else pltpu.VMEM(s, jnp.float32) for s in scratch],
        compiler_params=pltpu.CompilerParams(vmem_limit_bytes=VMEM_LIMIT),
    )(*inputs)


def placed(kernel, *axes):
    def with_place(*refs):
        where = [f(a) for a in axes for f in (lax.axis_index, lax.axis_size)]
        kernel(*where, *refs)

    return with_place


def on_device(
    source_field, adjoint_source, material, density, eps_inf, omega_dt, gamma_dt, delta_eps
):
    source = source_field.reshape(3, 16, 2, 8, 128)
    adjoint = adjoint_source.reshape(3, 16, 2, 8, 128)
    material = material.reshape(16, 2, 8, 128)
    params = (eps_inf, omega_dt, gamma_dt, delta_eps)
    arrays = (source, adjoint, material, density)
    y_low, y_high, source, adjoint, material, density = call(
        pack_kernel,
        [(7, 8, 8, 128)] * 2 + [jax.ShapeDtypeStruct(a.shape, a.dtype) for a in arrays],
        arrays,
        [pltpu.SemaphoreType.DMA((4,))],
        hbm=True,
    )
    y_next_in, y_before_in = round_trip(y_low, "dev", -1), round_trip(y_high, "dev", 1)
    (gains,) = call(medium_kernel, [(4, 16, 2, 8, 128)], (material, density, *params), tables=4)
    halo, x_low, x_high = call(
        placed(edge_kernel, "dev"),
        [(7, 16, 8, 128)] + [(85, 8, 128)] * 2,
        (y_next_in, y_before_in, source, adjoint, material, density),
    )
    x_next_in, x_before_in = round_trip(x_low, "grp", -1), round_trip(x_high, "grp", 1)
    state = call(
        placed(inner_kernel, "dev"),
        [STATE] * 4 + [(4, 16, 8, 128), (16, 8, 128)],
        (source, adjoint, halo, density, gains, *params),
        tables=4,
    )
    *fields, halo_gains, acc = state
    outer = (2, 3, 17, 3, 8, 128)
    final_field, partial = call(
        placed(outer_kernel, "dev", "grp"),
        [(3, 16, 2, 8, 128), (16, 128)],
        (*fields, gains, halo_gains, acc, x_next_in, x_before_in, *params),
        [outer] * 4 + [(4, 8, 3, 8, 128), (8, 8, 128)],
        4,
    )
    received = lax.all_to_all(partial, "dev", split_axis=0, concat_axis=0, tiled=True)
    across = source_field.shape[2] * lax.axis_size("dev")

    def total(received, out):
        sum_kernel(1.0 / math.sqrt(across), received, out)

    (shared,) = call(total, [(8, 16)], (received,))
    return final_field.reshape(source_field.shape), shared.T


def solution(mesh):
    in_specs = (
        P(None, "grp", "dev", None),
        P(None, "grp", "dev", None),
        P("grp", "dev", None),
        P("grp", None),
        P(),
        P(),
        P(),
        P(),
    )
    out_specs = (P(None, "grp", "dev", None), P("grp", "dev"))
    return jax.shard_map(
        on_device, mesh=mesh, in_specs=in_specs, out_specs=out_specs, check_vma=False
    )
```

```python
import math

import jax
import jax.numpy as jnp
from jax import lax
from jax.experimental import pallas as pl
from jax.experimental.pallas import tpu as pltpu
from jax.sharding import PartitionSpec as P

STEPS = 4
MATERIALS = 4
WIDE = 4
CHUNK = 4
VMEM_LIMIT = 24 * 1024 * 1024

TILES = range(3)
STATE = (2, 3, 16, 3, 8, 128)


def round_trip(value, axis, steps):
    count = lax.axis_size(axis)
    return lax.ppermute(value, axis, [(s, (s + steps) % count) for s in range(count)])


def iota(dim):
    return lax.broadcasted_iota(jnp.int32, (8, 128), dim)


def turned(value, by, dim):
    return pltpu.roll(value, by % value.shape[dim], dim)


def y_next(tiles):
    last = iota(0) == 7
    rolled = [turned(t, -1, 0) for t in tiles]
    return [jnp.where(last, rolled[(k + 1) % 3], rolled[k]) for k in TILES]


def y_before(tiles, inside):
    first = iota(0) == 0
    rolled = [turned(t, 1, 0) for t in tiles]
    edge = [rolled[2] * inside, rolled[0], rolled[1]]
    return [jnp.where(first, edge[k], rolled[k]) for k in TILES]


def z_next(tiles):
    last = iota(1) == 127
    return [jnp.where(last, 0.0, turned(t, -1, 1)) for t in tiles]


def z_before(tiles):
    first = iota(1) == 0
    return [jnp.where(first, 0.0, turned(t, 1, 1)) for t in tiles]


def loop(low, high, body, chunk=CHUNK):
    whole = (high - low) // chunk
    if whole:

        @pl.loop(0, whole)
        def _(k):
            for u in range(chunk):
                body(low + k * chunk + u)

    for plane in range(low + whole * chunk, high):
        body(plane)


def magnetic_plane(x, first, E, H, put):
    for run in range(2):
        ex, ey, ez = (E(run, c, x) for c in range(3))
        ey_x, ez_x = (E(run, c, x + 1) for c in (1, 2))
        ex_y, ez_y, ex_z, ey_z = y_next(ex), y_next(ez), z_next(ex), z_next(ey)
        olds = None if first else [H(run, c, x) for c in range(3)]
        for t in TILES:
            curl = (
                (ez_y[t] - ez[t]) - (ey_z[t] - ey[t]),
                (ex_z[t] - ex[t]) - (ez_x[t] - ez[t]),
                (ey_x[t] - ey[t]) - (ex_y[t] - ex[t]),
            )
            for c in range(3):
                put(run, c, x, t, -curl[c] if first else olds[c][t] - curl[c])


def electric_plane(x, step, E, H, now, old, gains, before_y, put_e, put_p):
    first, last = step == 1, step == STEPS
    fresh = []
    for run in range(2):
        hx, hy, hz = (H(run, c, x) for c in range(3))
        hy_x, hz_x = (H(run, c, x - 1) for c in (1, 2))
        hx_y, hz_y = y_before(hx, before_y), y_before(hz, before_y)
        hx_z, hy_z = z_before(hx), z_before(hy)
        es = [E(run, c, x) for c in range(3)]
        ps = None if first else [old(run, c, x) for c in range(3)]
        qs = None if step <= 2 else [now(run, c, x) for c in range(3)]
        mine = []
        for t in range(2) if last else TILES:
            curl = (
                (hz[t] - hz_y[t]) - (hy[t] - hy_z[t]),
                (hx[t] - hx_z[t]) - (hz[t] - hz_x[t]),
                (hy[t] - hy_x[t]) - (hx[t] - hx_y[t]),
            )
            for c in range(3):
                update = gains[2][t] * es[c][t]
                if first:
                    moved = update
                else:
                    update = gains[0][t] * ps[c][t] + update
                    if step > 2:
                        update = update + gains[1][t] * qs[c][t]
                    moved = update - ps[c][t]
                e = es[c][t] + (curl[c] - moved) * gains[3][t]
                put_e(run, c, x, t, e)
                if not last:
                    put_p(run, c, x, t, update)
                if t < 2:
                    mine.append(e)
        fresh.append(mine)
    products = None
    for f, a in zip(*fresh):
        products = f * a if products is None else products + f * a
    return products


def tables_of(eps_inf, omega_dt, gamma_dt, delta_eps):
    tables = []
    for m in range(MATERIALS):
        w, g = (jnp.full((8, 128), ref[m], jnp.float32) for ref in (omega_dt, gamma_dt))
        d, e = (jnp.full((8, 128), ref[m], jnp.float32) for ref in (delta_eps, eps_inf))
        squared, damping = w * w, g * 0.5
        tables.append(
            (
                (2.0 - squared) / (1.0 + damping),
                -(1.0 - damping) / (1.0 + damping),
                4.0 * (d * squared / (1.0 + damping)),
                4.0 * e,
            )
        )
    return tables


def medium(tables, number, layer, inside=None):
    picked = list(tables[0])
    for m in range(1, MATERIALS):
        here = number == m
        picked = [jnp.where(here, t, p) for t, p in zip(tables[m], picked)]
    inverse = 1.0 / (picked[3] + 8.0 * layer)
    if inside is not None:
        inverse = jnp.where(inside, inverse, 0.0)
    return picked[0], picked[1], picked[2], inverse


def y_inside(dev, devs):
    above, below = (dev < devs - 1).astype(jnp.int32), (dev > 0).astype(jnp.int32)
    return jnp.where(iota(0) >= 4, below, above) > 0


def layer_of(ref, *index):
    return jnp.broadcast_to(ref[index], (8, 128))


def pack_kernel(
    source_hbm, adjoint_hbm, material_hbm, density_hbm,
    y_low, y_high, x_low, x_high, source, adjoint, material, density, sems,
):
    pairs = ((source_hbm, source), (adjoint_hbm, adjoint), (material_hbm, material), (density_hbm, density))
    copies = [pltpu.make_async_copy(s, d, sems.at[k]) for k, (s, d) in enumerate(pairs)]
    for copy in copies:
        copy.start()
    for copy in copies:
        copy.wait()
    upper = iota(0) >= 4
    for slot in range(7):
        for pair in range(8):
            even, odd = (field_of(source, adjoint, material, slot, 2 * pair + k, 0) for k in range(2))
            y_low[slot, pair] = jnp.where(upper, turned(odd, 4, 0), even)
            even, odd = (field_of(source, adjoint, material, slot, 2 * pair + k, 1) for k in range(2))
            y_high[slot, pair] = jnp.where(upper, even, turned(odd, 4, 0))
        for k in range(WIDE):
            for tile in range(2):
                x_low[slot * 8 + k * 2 + tile] = field_of(source, adjoint, material, slot, k, tile)
                x_high[slot * 8 + k * 2 + tile] = field_of(source, adjoint, material, slot, 12 + k, tile)
    x_low[56] = density[0:8]
    x_high[56] = turned(density[8:16], 4, 0)


def field_of(source, adjoint, material, slot, plane, tile):
    if slot < 3:
        return source[slot, plane, tile]
    if slot < 6:
        return adjoint[slot - 3, plane, tile]
    return material[plane, tile].astype(jnp.float32)


def medium_kernel(material, density, eps_inf, omega_dt, gamma_dt, delta_eps, G):
    tables = tables_of(eps_inf, omega_dt, gamma_dt, delta_eps)

    @pl.loop(0, 16)
    def _(x):
        layer = layer_of(density, pl.ds(x, 1))
        for tile in range(2):
            for k, value in enumerate(medium(tables, material[x, tile], layer)):
                G[k, x, tile] = value


def corner_kernel(place, count, from_next, from_before, halo, c_low, c_high):
    upper = iota(0) >= 4
    for slot in range(7):
        for pair in range(8):
            ahead = jnp.where(place < count - 1, from_next[slot, pair], 0.0)
            behind = jnp.where(place > 0, from_before[slot, pair], 0.0)
            even = jnp.where(upper, behind, ahead)
            odd = turned(jnp.where(upper, ahead, behind), 4, 0)
            for plane, value in ((2 * pair, even), (2 * pair + 1, odd)):
                halo[slot, plane] = value
                if plane < WIDE:
                    c_low[slot, plane] = value
                if plane >= 12:
                    c_high[slot, plane - 12] = value


def inner_kernel(
    dev, devs,
    source, adjoint, halo, density, G, eps_inf, omega_dt, gamma_dt, delta_eps,
    E, H, PA, PB, G2, acc,
):
    tables = tables_of(eps_inf, omega_dt, gamma_dt, delta_eps)
    inside = y_inside(dev, devs)
    fields = (source, adjoint)

    @pl.loop(0, 16)
    def _(x):
        for run in range(2):
            for c in range(3):
                for tile in range(2):
                    E[run, c, x, tile] = fields[run][c, x, tile]
                E[run, c, x, 2] = halo[3 * run + c, x]
        layer = layer_of(density, pl.ds(x, 1))
        for k, value in enumerate(medium(tables, halo[6, x].astype(jnp.int32), layer, inside)):
            G2[k, x] = value

    acc[...] = jnp.zeros_like(acc)
    before_y = jnp.full((8, 128), (dev > 0).astype(jnp.float32))

    def reader(ref):
        return lambda run, c, x: [ref[run, c, x, t] for t in TILES]

    def writer(ref):
        def put(run, c, x, t, value):
            ref[run, c, x, t] = value

        return put

    for step in range(1, STEPS + 1):
        now, old = (PB, PA) if step % 2 == 0 else (PA, PB)

        def magnetic(x):
            magnetic_plane(x, step == 1, reader(E), reader(H), writer(H))

        def electric(x):
            gains = [[G[k, x, 0], G[k, x, 1], G2[k, x]] for k in range(4)]
            acc[x] += electric_plane(
                x, step, reader(E), reader(H), reader(now), reader(old), gains, before_y, writer(E), writer(now)
            )

        loop(step - 1, 16 - step, magnetic)
        loop(step, 16 - step, electric)


def outer_kernel(
    dev, devs, grp, grps,
    E_in, H_in, PA_in, PB_in, G, G2, acc,
    from_next, from_before, c_next, c_before, eps_inf, omega_dt, gamma_dt, delta_eps,
    final_field, partial, E, H, PA, PB, GO, sums,
):
    tables = tables_of(eps_inf, omega_dt, gamma_dt, delta_eps)
    y_in = y_inside(dev, devs)
    before_y = jnp.full((8, 128), (dev > 0).astype(jnp.float32))
    before_x = jnp.full((8, 128), (grp > 0).astype(jnp.float32))
    low_in, high_in = grp > 0, grp < grps - 1

    def slot_of(x):
        return x + 4 if x < 8 else x - 3

    for side in range(2):
        main, corner, x_in = ((from_before, c_before, low_in), (from_next, c_next, high_in))[side]
        for k in range(WIDE):
            x = 16 * side + k - (0 if side else 4)
            layer = layer_of(main, 56, pl.ds(k, 1))
            for t in TILES:
                number = corner[6, k] if t == 2 else main[48 + k * 2 + t]
                ok = jnp.logical_and(y_in, x_in) if t == 2 else x_in
                for n, value in enumerate(medium(tables, number.astype(jnp.int32), layer, ok)):
                    GO[n, side * 4 + k, t] = value

    def start(run, c, x):
        main, corner, x_in, k = (from_before, c_before, low_in, x + 4) if x < 0 else (from_next, c_next, high_in, x - 16)
        slot = 3 * run + c
        tiles = [main[slot * 8 + k * 2 + t] for t in range(2)] + [corner[slot, k]]
        return [jnp.where(x_in, t, 0.0) for t in tiles]

    for step in range(1, STEPS + 1):
        now, old, now_in, old_in = (PB, PA, PB_in, PA_in) if step % 2 == 0 else (PA, PB, PA_in, PB_in)

        def reader(mine, theirs, x_low, x_high):
            def read(run, c, x):
                if x_low <= x < x_high:
                    return [theirs[run, c, x, t] for t in TILES]
                if mine is E and step == 1:
                    return start(run, c, x)
                return [mine[run, c, slot_of(x), t] for t in TILES]

            return read

        def writer(ref):
            def put(run, c, x, t, value):
                ref[run, c, slot_of(x), t] = value

            return put

        def put_final(run, c, x, t, value):
            if run == 0:
                final_field[c, x, t] = value

        read_e = reader(E, E_in, step - 1, 17 - step)
        h_before = reader(H, H_in, max(step - 2, 0), 17 - step)
        h_after = reader(H, H_in, step - 1, 16 - step)
        read_now, read_old = reader(now, now_in, step - 2, 18 - step), reader(old, old_in, step - 1, 17 - step)

        for x in (*range(step - 5, step - 1), *range(16 - step, 20 - step)):
            magnetic_plane(x, step == 1, read_e, h_before, writer(H))
        for run in range(2):
            for c in (1, 2):
                for t in TILES:
                    H[run, c, slot_of(-1), t] = H[run, c, slot_of(-1), t] * before_x
        for x in (*range(step - 4, step), *range(16 - step, 20 - step)):
            if 0 <= x < 16:
                gains = [[G[k, x, 0], G[k, x, 1], G2[k, x]] for k in range(4)]
            else:
                gains = [[GO[k, x + 4 if x < 0 else x - 12, t] for t in TILES] for k in range(4)]
            put_e = put_final if step == STEPS else writer(E)
            products = electric_plane(
                x, step, read_e, h_after, read_now, read_old, gains, before_y, put_e, writer(now)
            )
            if 0 <= x < 16:
                k = x if x < 8 else x - 8
                sums[k] = products + (acc[x] if step in (x + 1, 16 - x) else sums[k])

    for c in range(3):
        for x in range(4, 12):
            for t in range(2):
                final_field[c, x, t] = E_in[0, c, x, t]

    whole = jnp.concatenate([sums[0:4], acc[4:12], sums[4:8]], axis=0)
    table = jnp.concatenate([jnp.sum(whole, axis=1), jnp.zeros((112, 128), jnp.float32)], axis=0)
    blocks = table.T.reshape(16, 8, 128)
    partial[...] = jnp.sum(pltpu.roll(blocks, 0, 2, stride=16, stride_axis=1), axis=1)


def sum_kernel(scale, received, field, out, field_out, sem):
    copy = pltpu.make_async_copy(field, field_out, sem)
    copy.start()
    row = jnp.broadcast_to(jnp.sum(received[...], axis=0, keepdims=True) * scale, (8, 128))
    table = row
    for z in range(1, 8):
        table = jnp.where(iota(0) == z, turned(row, -16 * z, 1), table)
    out[...] = table[:, 0:16]
    copy.wait()


def call(kernel, out_shapes, inputs, scratch=(), tables=0, hbm=False, out_hbm=()):
    vmem, smem = pl.BlockSpec(memory_space=pltpu.VMEM), pl.BlockSpec(memory_space=pltpu.SMEM)
    where = pl.BlockSpec(memory_space=pltpu.HBM) if hbm else vmem
    if hbm:
        inputs = [pltpu.with_memory_space_constraint(x, pltpu.HBM) for x in inputs]
    return pl.pallas_call(
        kernel,
        out_shape=[jax.ShapeDtypeStruct(s, jnp.float32) if isinstance(s, tuple) else s for s in out_shapes],
        in_specs=[where] * (len(inputs) - tables) + [smem] * tables,
        out_specs=[pl.BlockSpec(memory_space=pltpu.HBM) if k in out_hbm else vmem for k in range(len(out_shapes))],
        scratch_shapes=[s if not isinstance(s, tuple) else pltpu.VMEM(s, jnp.float32) for s in scratch],
        compiler_params=pltpu.CompilerParams(vmem_limit_bytes=VMEM_LIMIT),
    )(*inputs)


def placed(kernel, *axes):
    def with_place(*refs):
        where = [f(a) for a in axes for f in (lax.axis_index, lax.axis_size)]
        kernel(*where, *refs)

    return with_place


def on_device(
    source_field, adjoint_source, material, density, eps_inf, omega_dt, gamma_dt, delta_eps
):
    source = source_field.reshape(3, 16, 2, 8, 128)
    adjoint = adjoint_source.reshape(3, 16, 2, 8, 128)
    material = material.reshape(16, 2, 8, 128)
    params = (eps_inf, omega_dt, gamma_dt, delta_eps)
    arrays = (source, adjoint, material, density)
    y_low, y_high, x_low, x_high, source, adjoint, material, density = call(
        pack_kernel,
        [(7, 8, 8, 128)] * 2 + [(57, 8, 128)] * 2 + [jax.ShapeDtypeStruct(a.shape, a.dtype) for a in arrays],
        arrays,
        [pltpu.SemaphoreType.DMA((4,))],
        hbm=True,
    )
    y_next_in, y_before_in = round_trip(y_low, "dev", -1), round_trip(y_high, "dev", 1)
    x_next_in, x_before_in = round_trip(x_low, "grp", -1), round_trip(x_high, "grp", 1)
    (gains,) = call(medium_kernel, [(4, 16, 2, 8, 128)], (material, density, *params), tables=4)
    halo, c_low, c_high = call(
        placed(corner_kernel, "dev"),
        [(7, 16, 8, 128)] + [(7, 4, 8, 128)] * 2,
        (y_next_in, y_before_in),
    )
    c_next_in, c_before_in = round_trip(c_low, "grp", -1), round_trip(c_high, "grp", 1)
    state = call(
        placed(inner_kernel, "dev"),
        [STATE] * 4 + [(4, 16, 8, 128), (16, 8, 128)],
        (source, adjoint, halo, density, gains, *params),
        tables=4,
    )
    *fields, halo_gains, acc = state
    outer = (2, 3, 17, 3, 8, 128)
    final_field, partial = call(
        placed(outer_kernel, "dev", "grp"),
        [(3, 16, 2, 8, 128), (16, 128)],
        (*fields, gains, halo_gains, acc, x_next_in, x_before_in, c_next_in, c_before_in, *params),
        [outer] * 4 + [(4, 8, 3, 8, 128), (8, 8, 128)],
        4,
    )
    received = lax.all_to_all(partial, "dev", split_axis=0, concat_axis=0, tiled=True)
    across = source_field.shape[2] * lax.axis_size("dev")

    def total(*refs):
        sum_kernel(1.0 / math.sqrt(across), *refs)

    shared, final_field = call(
        total,
        [(8, 16), final_field.shape],
        (received, final_field),
        [pltpu.SemaphoreType.DMA(())],
        out_hbm=(1,),
    )
    return final_field.reshape(source_field.shape), shared.T


def solution(mesh):
    in_specs = (
        P(None, "grp", "dev", None),
        P(None, "grp", "dev", None),
        P("grp", "dev", None),
        P("grp", None),
        P(),
        P(),
        P(),
        P(),
    )
    out_specs = (P(None, "grp", "dev", None), P("grp", "dev"))
    return jax.shard_map(
        on_device, mesh=mesh, in_specs=in_specs, out_specs=out_specs, check_vma=False
    )
```

```python
import math

import jax
import jax.numpy as jnp
from jax import lax
from jax.experimental import pallas as pl
from jax.experimental.pallas import tpu as pltpu
from jax.sharding import PartitionSpec as P

STEPS = 4
MATERIALS = 4
WIDE = 4
CHUNK = 4
VMEM_LIMIT = 24 * 1024 * 1024

TILES = range(3)
STATE = (2, 3, 16, 3, 8, 128)


def round_trip(value, axis, steps):
    count = lax.axis_size(axis)
    return lax.ppermute(value, axis, [(s, (s + steps) % count) for s in range(count)])


def iota(dim):
    return lax.broadcasted_iota(jnp.int32, (8, 128), dim)


def turned(value, by, dim):
    return pltpu.roll(value, by % value.shape[dim], dim)


def y_next(tiles):
    last = iota(0) == 7
    rolled = [turned(t, -1, 0) for t in tiles]
    return [jnp.where(last, rolled[(k + 1) % 3], rolled[k]) for k in TILES]


def y_before(tiles, inside):
    first = iota(0) == 0
    rolled = [turned(t, 1, 0) for t in tiles]
    edge = [rolled[2] * inside, rolled[0], rolled[1]]
    return [jnp.where(first, edge[k], rolled[k]) for k in TILES]


def z_next(tiles):
    last = iota(1) == 127
    return [jnp.where(last, 0.0, turned(t, -1, 1)) for t in tiles]


def z_before(tiles):
    first = iota(1) == 0
    return [jnp.where(first, 0.0, turned(t, 1, 1)) for t in tiles]


def loop(low, high, body, chunk=CHUNK):
    whole = (high - low) // chunk
    if whole:

        @pl.loop(0, whole)
        def _(k):
            for u in range(chunk):
                body(low + k * chunk + u)

    for plane in range(low + whole * chunk, high):
        body(plane)


def magnetic_plane(x, first, E, H, put):
    for run in range(2):
        ex, ey, ez = (E(run, c, x) for c in range(3))
        ey_x, ez_x = (E(run, c, x + 1) for c in (1, 2))
        ex_y, ez_y, ex_z, ey_z = y_next(ex), y_next(ez), z_next(ex), z_next(ey)
        olds = None if first else [H(run, c, x) for c in range(3)]
        for t in TILES:
            curl = (
                (ez_y[t] - ez[t]) - (ey_z[t] - ey[t]),
                (ex_z[t] - ex[t]) - (ez_x[t] - ez[t]),
                (ey_x[t] - ey[t]) - (ex_y[t] - ex[t]),
            )
            for c in range(3):
                put(run, c, x, t, -curl[c] if first else olds[c][t] - curl[c])


def electric_plane(x, step, E, H, now, old, gains, before_y, put_e, put_p):
    first, last = step == 1, step == STEPS
    fresh = []
    for run in range(2):
        hx, hy, hz = (H(run, c, x) for c in range(3))
        hy_x, hz_x = (H(run, c, x - 1) for c in (1, 2))
        hx_y, hz_y = y_before(hx, before_y), y_before(hz, before_y)
        hx_z, hy_z = z_before(hx), z_before(hy)
        es = [E(run, c, x) for c in range(3)]
        ps = None if first else [old(run, c, x) for c in range(3)]
        qs = None if step <= 2 else [now(run, c, x) for c in range(3)]
        mine = []
        for t in range(2) if last else TILES:
            curl = (
                (hz[t] - hz_y[t]) - (hy[t] - hy_z[t]),
                (hx[t] - hx_z[t]) - (hz[t] - hz_x[t]),
                (hy[t] - hy_x[t]) - (hx[t] - hx_y[t]),
            )
            for c in range(3):
                update = gains[2][t] * es[c][t]
                if first:
                    moved = update
                else:
                    update = gains[0][t] * ps[c][t] + update
                    if step > 2:
                        update = update + gains[1][t] * qs[c][t]
                    moved = update - ps[c][t]
                e = es[c][t] + (curl[c] - moved) * gains[3][t]
                put_e(run, c, x, t, e)
                if not last:
                    put_p(run, c, x, t, update)
                if t < 2:
                    mine.append(e)
        fresh.append(mine)
    products = None
    for f, a in zip(*fresh):
        products = f * a if products is None else products + f * a
    return products


def tables_of(eps_inf, omega_dt, gamma_dt, delta_eps):
    tables = []
    for m in range(MATERIALS):
        w, g = (jnp.full((8, 128), ref[m], jnp.float32) for ref in (omega_dt, gamma_dt))
        d, e = (jnp.full((8, 128), ref[m], jnp.float32) for ref in (delta_eps, eps_inf))
        squared, damping = w * w, g * 0.5
        tables.append(
            (
                (2.0 - squared) / (1.0 + damping),
                -(1.0 - damping) / (1.0 + damping),
                4.0 * (d * squared / (1.0 + damping)),
                4.0 * e,
            )
        )
    return tables


def read_tables(table):
    return [[table[m, k] for k in range(4)] for m in range(MATERIALS)]


def medium(tables, number, layer, inside=None):
    picked = list(tables[0])
    for m in range(1, MATERIALS):
        here = number == m
        picked = [jnp.where(here, t, p) for t, p in zip(tables[m], picked)]
    inverse = 1.0 / (picked[3] + 8.0 * layer)
    if inside is not None:
        inverse = jnp.where(inside, inverse, 0.0)
    return picked[0], picked[1], picked[2], inverse


def y_inside(dev, devs):
    above, below = (dev < devs - 1).astype(jnp.int32), (dev > 0).astype(jnp.int32)
    return jnp.where(iota(0) >= 4, below, above) > 0


def layer_of(ref, *index):
    return jnp.broadcast_to(ref[index], (8, 128))


def pack_kernel(
    source_hbm, adjoint_hbm, material_hbm, density_hbm, eps_hbm, omega_hbm, gamma_hbm, delta_hbm,
    y_low, y_high, x_low, x_high, source, adjoint, material, density, table,
    eps_inf, omega_dt, gamma_dt, delta_eps, sems,
):
    pairs = (
        (source_hbm, source), (adjoint_hbm, adjoint), (material_hbm, material), (density_hbm, density),
        (eps_hbm, eps_inf), (omega_hbm, omega_dt), (gamma_hbm, gamma_dt), (delta_hbm, delta_eps),
    )
    copies = [pltpu.make_async_copy(s, d, sems.at[k]) for k, (s, d) in enumerate(pairs)]
    for copy in copies:
        copy.start()
    for copy in copies:
        copy.wait()
    upper = iota(0) >= 4
    for slot in range(7):
        for pair in range(8):
            even, odd = (field_of(source, adjoint, material, slot, 2 * pair + k, 0) for k in range(2))
            y_low[slot, pair] = jnp.where(upper, turned(odd, 4, 0), even)
            even, odd = (field_of(source, adjoint, material, slot, 2 * pair + k, 1) for k in range(2))
            y_high[slot, pair] = jnp.where(upper, even, turned(odd, 4, 0))
        for k in range(WIDE):
            for tile in range(2):
                x_low[slot * 8 + k * 2 + tile] = field_of(source, adjoint, material, slot, k, tile)
                x_high[slot * 8 + k * 2 + tile] = field_of(source, adjoint, material, slot, 12 + k, tile)
    x_low[56] = density[0:8]
    x_high[56] = turned(density[8:16], 4, 0)
    for m, values in enumerate(tables_of(eps_inf, omega_dt, gamma_dt, delta_eps)):
        for k, value in enumerate(values):
            table[m, k] = value


def field_of(source, adjoint, material, slot, plane, tile):
    if slot < 3:
        return source[slot, plane, tile]
    if slot < 6:
        return adjoint[slot - 3, plane, tile]
    return material[plane, tile].astype(jnp.float32)


def medium_kernel(material, density, table, G):
    tables = read_tables(table)

    @pl.loop(0, 16)
    def _(x):
        layer = layer_of(density, pl.ds(x, 1))
        for tile in range(2):
            for k, value in enumerate(medium(tables, material[x, tile], layer)):
                G[k, x, tile] = value


def corner_kernel(place, count, from_next, from_before, gains, halo, c_low, c_high):
    upper = iota(0) >= 4
    for slot in range(7):
        for pair in range(8):
            ahead = jnp.where(place < count - 1, from_next[slot, pair], 0.0)
            behind = jnp.where(place > 0, from_before[slot, pair], 0.0)
            even = jnp.where(upper, behind, ahead)
            odd = turned(jnp.where(upper, ahead, behind), 4, 0)
            for plane, value in ((2 * pair, even), (2 * pair + 1, odd)):
                halo[slot, plane] = value
                if plane < WIDE:
                    c_low[slot, plane] = value
                if plane >= 12:
                    c_high[slot, plane - 12] = value


def inner_kernel(
    dev, devs,
    source, adjoint, halo, density, G, table,
    E, H, PA, PB, G2, acc,
):
    tables = read_tables(table)
    inside = y_inside(dev, devs)
    fields = (source, adjoint)

    @pl.loop(0, 16)
    def _(x):
        for run in range(2):
            for c in range(3):
                for tile in range(2):
                    E[run, c, x, tile] = fields[run][c, x, tile]
                E[run, c, x, 2] = halo[3 * run + c, x]
        layer = layer_of(density, pl.ds(x, 1))
        for k, value in enumerate(medium(tables, halo[6, x].astype(jnp.int32), layer, inside)):
            G2[k, x] = value

    acc[...] = jnp.zeros_like(acc)
    before_y = jnp.full((8, 128), (dev > 0).astype(jnp.float32))

    def reader(ref):
        return lambda run, c, x: [ref[run, c, x, t] for t in TILES]

    def writer(ref):
        def put(run, c, x, t, value):
            ref[run, c, x, t] = value

        return put

    for step in range(1, STEPS + 1):
        now, old = (PB, PA) if step % 2 == 0 else (PA, PB)

        def magnetic(x):
            magnetic_plane(x, step == 1, reader(E), reader(H), writer(H))

        def electric(x):
            gains = [[G[k, x, 0], G[k, x, 1], G2[k, x]] for k in range(4)]
            acc[x] += electric_plane(
                x, step, reader(E), reader(H), reader(now), reader(old), gains, before_y, writer(E), writer(now)
            )

        loop(step - 1, 16 - step, magnetic)
        loop(step, 16 - step, electric)


def outer_kernel(
    dev, devs, grp, grps,
    E_in, H_in, PA_in, PB_in, G, G2, acc,
    from_next, from_before, c_next, c_before, table,
    final_field, partial, E, H, PA, PB, GO, sums,
):
    tables = read_tables(table)
    y_in = y_inside(dev, devs)
    before_y = jnp.full((8, 128), (dev > 0).astype(jnp.float32))
    before_x = jnp.full((8, 128), (grp > 0).astype(jnp.float32))
    low_in, high_in = grp > 0, grp < grps - 1

    def slot_of(x):
        return x + 4 if x < 8 else x - 3

    for side in range(2):
        main, corner, x_in = ((from_before, c_before, low_in), (from_next, c_next, high_in))[side]
        for k in range(WIDE):
            x = 16 * side + k - (0 if side else 4)
            layer = layer_of(main, 56, pl.ds(k, 1))
            for t in TILES:
                number = corner[6, k] if t == 2 else main[48 + k * 2 + t]
                ok = jnp.logical_and(y_in, x_in) if t == 2 else x_in
                for n, value in enumerate(medium(tables, number.astype(jnp.int32), layer, ok)):
                    GO[n, side * 4 + k, t] = value

    def start(run, c, x):
        main, corner, x_in, k = (from_before, c_before, low_in, x + 4) if x < 0 else (from_next, c_next, high_in, x - 16)
        slot = 3 * run + c
        tiles = [main[slot * 8 + k * 2 + t] for t in range(2)] + [corner[slot, k]]
        return [jnp.where(x_in, t, 0.0) for t in tiles]

    for step in range(1, STEPS + 1):
        now, old, now_in, old_in = (PB, PA, PB_in, PA_in) if step % 2 == 0 else (PA, PB, PA_in, PB_in)

        def reader(mine, theirs, x_low, x_high):
            def read(run, c, x):
                if x_low <= x < x_high:
                    return [theirs[run, c, x, t] for t in TILES]
                if mine is E and step == 1:
                    return start(run, c, x)
                return [mine[run, c, slot_of(x), t] for t in TILES]

            return read

        def writer(ref):
            def put(run, c, x, t, value):
                ref[run, c, slot_of(x), t] = value

            return put

        def put_final(run, c, x, t, value):
            if run == 0:
                final_field[c, x, t] = value

        read_e = reader(E, E_in, step - 1, 17 - step)
        h_before = reader(H, H_in, max(step - 2, 0), 17 - step)
        h_after = reader(H, H_in, step - 1, 16 - step)
        read_now, read_old = reader(now, now_in, step - 2, 18 - step), reader(old, old_in, step - 1, 17 - step)

        for x in (*range(step - 5, step - 1), *range(16 - step, 20 - step)):
            magnetic_plane(x, step == 1, read_e, h_before, writer(H))
        for run in range(2):
            for c in (1, 2):
                for t in TILES:
                    H[run, c, slot_of(-1), t] = H[run, c, slot_of(-1), t] * before_x
        for x in (*range(step - 4, step), *range(16 - step, 20 - step)):
            if 0 <= x < 16:
                gains = [[G[k, x, 0], G[k, x, 1], G2[k, x]] for k in range(4)]
            else:
                gains = [[GO[k, x + 4 if x < 0 else x - 12, t] for t in TILES] for k in range(4)]
            put_e = put_final if step == STEPS else writer(E)
            products = electric_plane(
                x, step, read_e, h_after, read_now, read_old, gains, before_y, put_e, writer(now)
            )
            if 0 <= x < 16:
                k = x if x < 8 else x - 8
                sums[k] = products + (acc[x] if step in (x + 1, 16 - x) else sums[k])

    for c in range(3):
        for x in range(4, 12):
            for t in range(2):
                final_field[c, x, t] = E_in[0, c, x, t]

    whole = jnp.concatenate([sums[0:4], acc[4:12], sums[4:8]], axis=0)
    table = jnp.concatenate([jnp.sum(whole, axis=1), jnp.zeros((112, 128), jnp.float32)], axis=0)
    blocks = table.T.reshape(16, 8, 128)
    partial[...] = jnp.sum(pltpu.roll(blocks, 0, 2, stride=16, stride_axis=1), axis=1)


def sum_kernel(scale, received, field, out, field_out, sem):
    copy = pltpu.make_async_copy(field, field_out, sem)
    copy.start()
    row = jnp.broadcast_to(jnp.sum(received[...], axis=0, keepdims=True) * scale, (8, 128))
    table = row
    for z in range(1, 8):
        table = jnp.where(iota(0) == z, turned(row, -16 * z, 1), table)
    out[...] = table[:, 0:16]
    copy.wait()


def call(kernel, out_shapes, inputs, scratch=(), hbm=False, out_hbm=()):
    vmem = pl.BlockSpec(memory_space=pltpu.VMEM)
    where = pl.BlockSpec(memory_space=pltpu.HBM) if hbm else vmem
    if hbm:
        inputs = [pltpu.with_memory_space_constraint(x, pltpu.HBM) for x in inputs]
    return pl.pallas_call(
        kernel,
        out_shape=[jax.ShapeDtypeStruct(s, jnp.float32) if isinstance(s, tuple) else s for s in out_shapes],
        in_specs=[where] * len(inputs),
        out_specs=[pl.BlockSpec(memory_space=pltpu.HBM) if k in out_hbm else vmem for k in range(len(out_shapes))],
        scratch_shapes=[s if not isinstance(s, tuple) else pltpu.VMEM(s, jnp.float32) for s in scratch],
        compiler_params=pltpu.CompilerParams(vmem_limit_bytes=VMEM_LIMIT),
    )(*inputs)


def placed(kernel, *axes):
    def with_place(*refs):
        where = [f(a) for a in axes for f in (lax.axis_index, lax.axis_size)]
        kernel(*where, *refs)

    return with_place


def on_device(
    source_field, adjoint_source, material, density, eps_inf, omega_dt, gamma_dt, delta_eps
):
    source = source_field.reshape(3, 16, 2, 8, 128)
    adjoint = adjoint_source.reshape(3, 16, 2, 8, 128)
    material = material.reshape(16, 2, 8, 128)
    arrays = (source, adjoint, material, density)
    y_low, y_high, x_low, x_high, source, adjoint, material, density, table = call(
        pack_kernel,
        [(7, 8, 8, 128)] * 2 + [(57, 8, 128)] * 2 + [jax.ShapeDtypeStruct(a.shape, a.dtype) for a in arrays] + [(4, 4, 8, 128)],
        (*arrays, eps_inf, omega_dt, gamma_dt, delta_eps),
        [pltpu.SMEM((4,), jnp.float32)] * 4 + [pltpu.SemaphoreType.DMA((8,))],
        hbm=True,
    )
    y_next_in, y_before_in = round_trip(y_low, "dev", -1), round_trip(y_high, "dev", 1)
    x_next_in, x_before_in = round_trip(x_low, "grp", -1), round_trip(x_high, "grp", 1)
    (gains,) = call(medium_kernel, [(4, 16, 2, 8, 128)], (material, density, table))
    halo, c_low, c_high = call(
        placed(corner_kernel, "dev"),
        [(7, 16, 8, 128)] + [(7, 4, 8, 128)] * 2,
        (y_next_in, y_before_in, gains),
    )
    c_next_in, c_before_in = round_trip(c_low, "grp", -1), round_trip(c_high, "grp", 1)
    state = call(
        placed(inner_kernel, "dev"),
        [STATE] * 4 + [(4, 16, 8, 128), (16, 8, 128)],
        (source, adjoint, halo, density, gains, table),
    )
    *fields, halo_gains, acc = state
    outer = (2, 3, 17, 3, 8, 128)
    final_field, partial = call(
        placed(outer_kernel, "dev", "grp"),
        [(3, 16, 2, 8, 128), (16, 128)],
        (*fields, gains, halo_gains, acc, x_next_in, x_before_in, c_next_in, c_before_in, table),
        [outer] * 4 + [(4, 8, 3, 8, 128), (8, 8, 128)],
    )
    received = lax.all_to_all(partial, "dev", split_axis=0, concat_axis=0, tiled=True)
    across = source_field.shape[2] * lax.axis_size("dev")

    def total(*refs):
        sum_kernel(1.0 / math.sqrt(across), *refs)

    shared, final_field = call(
        total,
        [(8, 16), final_field.shape],
        (received, final_field),
        [pltpu.SemaphoreType.DMA(())],
        out_hbm=(1,),
    )
    return final_field.reshape(source_field.shape), shared.T


def solution(mesh):
    in_specs = (
        P(None, "grp", "dev", None),
        P(None, "grp", "dev", None),
        P("grp", "dev", None),
        P("grp", None),
        P(),
        P(),
        P(),
        P(),
    )
    out_specs = (P(None, "grp", "dev", None), P("grp", "dev"))
    return jax.shard_map(
        on_device, mesh=mesh, in_specs=in_specs, out_specs=out_specs, check_vma=False
    )
```
